512 devices in a mesh: gx: 64 (over x_lo, z, core), gz: 8 (over y, x_hi).
Axes of the slice: x: 4 (x_hi: 2, x_lo: 2; x = x_hi * 2 + x_lo), y: 4, z: 16, core: 2. Of those that a mesh axis runs over, the one named last changes fastest.
Arguments:
- particle_drag: bfloat16 [64, 8, 4, 2048], P('gx', 'gz'), may hold values from -48 to 48
- particle_weights: bfloat16 [64, 8, 2048, 128], P('gx', 'gz'), may hold values from 0 to 1
- migration_counts: int32 [64, 8, 5], P('gx', 'gz'), may hold values from 0 to 1792, as said below
- tile_owner: int32 [64, 8, 384, 1], P('gx', 'gz'), may hold values from 0 to 8; in each aligned block of 384 rows (0 to 383, 384 to 767, ..., all dimensions but the last counted through in order) at most 128 rows name the same one
- tile_column: int32 [64, 8, 384], P('gx', 'gz'), may hold values from 0 to 1023
Outputs:
- filtered_source: float32 [2048, 256, 4, 128], P('gx', 'gz')
The draws below stay inside these ranges and needn't reach their ends.
Inputs may be any that keep to these rules, and one draw needn't show every extreme that they name: migration_counts[a, b, 0] is 2048 minus the other four; each of migration_counts[a, b, 1..4] is at most 256, and on every device one of them equals 256; on some device the other three are 0, so that it keeps 2048 - 256. `tile_owner`: on each device at most 128 tiles carry the same code, and on some device some code is carried by exactly 128 tiles.
All inputs are finite; a program needn't handle non-finite values.
Results may differ from the reference program's by a relative error of at most 0.00035.
Values may be sent and summed in bfloat16 or wider, within the bound.
A program may use at most 64 MiB of HBM per device.

```python
import math
import jax
import jax.numpy as jnp
import numpy as np
from jax import lax

CX = 32
CZ = 32
NY = 128
P_SIZE = 2048
G = 8
REACH = 4
M = 256
NTQ = 384
KT = 128
NX = 2048
NZ = 256
N_GX = 64
N_GZ = 8


def draw_migration_counts(key, part):
    own_key = jax.random.fold_in(key, 11)
    first_key, second_key = jax.random.split(own_key)
    moving = jax.random.randint(first_key, (N_GX, N_GZ, 4), 0, M + 1)
    full_side = jax.random.randint(second_key, (N_GX, N_GZ, 1), 0, 4)
    side_ids = jnp.arange(4)[None, None, :]
    first_device = (jnp.arange(N_GX)[:, None, None] == 0) & (jnp.arange(N_GZ)[None, :, None] == 0)
    moving = jnp.where(first_device, jnp.zeros_like(moving), moving)
    moving = jnp.where(side_ids == full_side, M, moving)
    staying = P_SIZE - jnp.sum(moving, axis=-1, keepdims=True)
    return jnp.concatenate([staying, moving], axis=-1).astype(jnp.int32)


def place_ends(array, key, low, top_value):
    extent = array.shape
    place = [jax.random.randint(jax.random.fold_in(key, axis), (), 0, extent[axis]) for axis in range(len(extent))]
    array = array.at[tuple(place)].set(low)
    longest = extent.index(max(extent))
    place[longest] = (place[longest] + 1) % extent[longest]
    return array.at[tuple(place)].set(top_value)


def levels(rng, extent, shards, smallest, top_value):
    factor_of, own = 1.0, jax.random.fold_in(rng, 6)
    for axis_at, shards_of in shards:
        heights = jnp.exp(jax.random.uniform(jax.random.fold_in(own, axis_at), (shards_of,), jnp.float32, smallest / len(shards), top_value / len(shards)))
        factor_of = factor_of * jnp.repeat(heights, extent[axis_at] // shards_of).reshape([-1 if axis == axis_at else 1 for axis in range(len(extent))])
    return factor_of


def deal_out(rng, own, number, rows, count, top, limit, slope):
    order = jax.random.permutation(rng, count)
    packed, usual = load_shares(count, rows * top, limit, slope, True), load_shares(count, rows * top, limit, slope, False)
    places = jnp.arange(count)

    def named(tallies, offset_by):
        used = int((tallies > 0).sum())
        fixed = max(1, used // 4)
        passed = fixed + (places - fixed + offset_by * (used - fixed)) % max(1, count - fixed)
        return jnp.zeros((count,), jnp.int32).at[order[jnp.where(places < fixed, places, passed)]].set(jnp.asarray(tallies, jnp.int32))

    tallies = jnp.where(number % 4 == 0, named(packed, number // 4), named(usual, number - number // 4 - 1))
    mixed = jax.random.permutation(jax.random.fold_in(own, 3), count)
    donor, receiver = mixed[0:count // 2 * 2:2], mixed[1:count // 2 * 2:2]
    room = jnp.minimum(tallies[donor] - 1, limit - tallies[receiver]) // 2
    room = jnp.where((donor == order[0]) | (receiver == order[0]) | (tallies[receiver] == 0), 0, jnp.maximum(room, 0))
    passed = jax.random.randint(jax.random.fold_in(own, 4), (count // 2,), 0, 1 << 20) % (room + 1)
    tallies = tallies.at[donor].add(-passed).at[receiver].add(passed)
    items = jnp.searchsorted(jnp.cumsum(tallies), jnp.arange(rows * top), side="right").astype(jnp.int32)
    table = items.reshape(top, rows).T
    table = table[jax.random.permutation(jax.random.fold_in(own, 1), rows)]
    offset_by = jax.random.randint(jax.random.fold_in(own, 2), (rows, 1), 0, top)
    return jnp.take_along_axis(table, (jnp.arange(top)[None, :] + offset_by) % top, axis=1)


def load_shares(amount, total, most, slope, full):
    loads = [(1 << 20) // math.isqrt(standing ** slope) + 1 for standing in range(1, amount + 1)]
    largest = most if full else min(most, max(-(-total // amount), total * loads[0] // sum(loads)))
    least = 1 if total - largest >= amount - 1 else 0
    holding, spare = [largest] + [least] * (amount - 1), total - largest - least * (amount - 1)
    while spare > 0:
        free = [i for i in range(1, amount) if holding[i] < largest] or [i for i in range(1, amount) if holding[i] < most]
        pool, budget = sum([loads[i] for i in free]), spare
        for i in free:
            extra = min(most - holding[i], max(1, budget * loads[i] // pool), spare)
            holding[i] = holding[i] + extra
            spare = spare - extra
    return np.array(holding)


def scatter_about(key, shape, width, bound, shards=(), kind=jnp.bfloat16):
    loudness = levels(key, shape, shards, -0.22, 0.18) if shards else 1.0
    array = jax.random.normal(key, shape, jnp.float32) * width * loudness
    return jnp.minimum(jnp.maximum(array, -bound), bound).astype(kind)


def setup_inputs(seed: int = 0) -> dict:
    splits = jax.random.split(jax.random.key(seed), 6)
    particle_drag = scatter_about(splits[0], (N_GX, N_GZ, 4, P_SIZE), 8.0, 48.0, ((0, 64), (1, 8)))
    particle_weights = jnp.clip(1.0 * jax.random.uniform(splits[1], (N_GX, N_GZ, P_SIZE, NY), jnp.float32) ** levels(splits[1], (N_GX, N_GZ, P_SIZE, NY), ((0, 64), (1, 8)), -0.2, 0.2), 0.0, 1.0).astype(jnp.bfloat16)
    migration_counts = draw_migration_counts(jax.random.fold_in(splits[5], 71), 0)
    tile_owner_keys = jax.random.split(jax.random.fold_in(splits[3], 1), N_GX * N_GZ * NTQ // NTQ)
    tile_owner_turns = jax.random.permutation(jax.random.fold_in(splits[3], 3), N_GX * N_GZ * NTQ // NTQ)
    tile_owner = jax.vmap(lambda own, number: deal_out(jax.random.fold_in(splits[3], 2), own, number, NTQ, 9, 1, KT, 2))(tile_owner_keys, tile_owner_turns).reshape((N_GX, N_GZ, NTQ, 1))
    tile_column = place_ends(jax.random.randint(splits[4], (N_GX, N_GZ, NTQ), 0, CX * CZ), jax.random.fold_in(splits[4], 1), 0, (CX * CZ) - 1).astype(jnp.int32)
    return dict(particle_drag=particle_drag, particle_weights=particle_weights, migration_counts=migration_counts, tile_owner=tile_owner, tile_column=tile_column)


def gauss_taps():
    raw_values = [math.exp(-offset_value * offset_value / 8.0) for offset_value in range(-REACH, REACH + 1)]
    total_value = sum(raw_values)
    return [raw_entry / total_value for raw_entry in raw_values]


def deposit_tiles(part_drag, part_weights):
    grid_rows = part_drag.shape[0]
    grid_cols = part_drag.shape[1]
    channel_count = part_drag.shape[2]
    groups_count = part_drag.shape[3] // G
    drag_groups = part_drag.astype(jnp.float32).reshape(grid_rows, grid_cols, channel_count, groups_count, G)
    weight_groups = part_weights.astype(jnp.float32).reshape(grid_rows, grid_cols, groups_count, G, NY)
    tiles_made = jnp.einsum("abctg,abtgy->abtcy", drag_groups, weight_groups, precision=lax.Precision.HIGHEST)
    return tiles_made.reshape(grid_rows, grid_cols, groups_count, channel_count * NY)


def reference(particle_drag, particle_weights, migration_counts, tile_owner, tile_column):
    channel_count = particle_drag.shape[2]
    starts_at = jnp.cumsum(migration_counts, axis=-1) - migration_counts
    slot_ids = jnp.arange(P_SIZE).astype(jnp.int32)
    keep_mask = slot_ids[None, None, None, :] < migration_counts[:, :, 0:1, None]
    kept_drag = jnp.where(keep_mask, particle_drag, jnp.zeros_like(particle_drag))
    tile_parts = [deposit_tiles(kept_drag, particle_weights)]
    lane_ids = jnp.arange(M).astype(jnp.int32)
    for direction, axis_index, roll_by in ((1, 0, 1), (2, 0, -1), (3, 1, 1), (4, 1, -1)):
        pick_ids = jnp.minimum(starts_at[:, :, direction:direction + 1] + lane_ids[None, None, :], P_SIZE - 1).astype(jnp.int32)
        live_mask = lane_ids[None, None, :] < migration_counts[:, :, direction:direction + 1]
        drag_index = jnp.broadcast_to(pick_ids[:, :, None, :], (N_GX, N_GZ, channel_count, M))
        sent_drag = jnp.take_along_axis(particle_drag, drag_index, axis=3)
        sent_drag = jnp.where(live_mask[:, :, None, :], sent_drag, jnp.zeros_like(sent_drag))
        weight_index = jnp.broadcast_to(pick_ids[:, :, :, None], (N_GX, N_GZ, M, NY))
        sent_weights = jnp.take_along_axis(particle_weights, weight_index, axis=2)
        moved_drag = jnp.roll(sent_drag, roll_by, axis=axis_index)
        moved_weights = jnp.roll(sent_weights, roll_by, axis=axis_index)
        tile_parts.append(deposit_tiles(moved_drag, moved_weights))
    all_tiles = jnp.concatenate(tile_parts, axis=2)
    owner_code = tile_owner[:, :, :, 0]
    step_x = owner_code // 3 - 1
    step_z = owner_code % 3 - 1
    home_x = jnp.arange(N_GX).astype(jnp.int32)[:, None, None]
    home_z = jnp.arange(N_GZ).astype(jnp.int32)[None, :, None]
    owner_x = (home_x + step_x) % N_GX
    owner_z = (home_z + step_z) % N_GZ
    cell_x = owner_x * CX + tile_column // CZ
    cell_z = owner_z * CZ + tile_column % CZ
    flat_cell = (cell_x * NZ + cell_z).reshape(-1).astype(jnp.int32)
    source_flat = jnp.zeros((NX * NZ, channel_count * NY), jnp.float32)
    source_flat = source_flat.at[flat_cell].add(all_tiles.reshape(-1, channel_count * NY))
    source_field = source_flat.reshape(NX, NZ, channel_count, NY)
    gauss_weights = gauss_taps()
    padded_y = jnp.pad(source_field, ((0, 0), (0, 0), (0, 0), (REACH, REACH)))
    along_y = jnp.zeros_like(source_field)
    for tap_index in range(2 * REACH + 1):
        along_y = along_y + gauss_weights[tap_index] * padded_y[:, :, :, tap_index:tap_index + NY]
    along_x = jnp.zeros_like(source_field)
    for tap_index in range(2 * REACH + 1):
        along_x = along_x + gauss_weights[tap_index] * jnp.roll(along_y, REACH - tap_index, axis=0)
    filtered_source = jnp.zeros_like(source_field)
    for tap_index in range(2 * REACH + 1):
        filtered_source = filtered_source + gauss_weights[tap_index] * jnp.roll(along_x, REACH - tap_index, axis=1)
    return filtered_source
```

```python
import math

import jax
import jax.numpy as jnp
from jax import lax
from jax.experimental import pallas as pl
from jax.experimental.pallas import tpu as pltpu
from jax.sharding import PartitionSpec as P

CX = 32
CZ = 32
NY = 128
CH = 4
P_SIZE = 2048
G = 8
REACH = 4
M = 256
KT = 128
NT = 384
F = CH * NY
COLS = CX * CZ
MESH = pl.DeviceIdType.MESH
f32, bf16, i32 = jnp.float32, jnp.bfloat16, jnp.int32
HIGHEST = lax.Precision.HIGHEST


def gauss_taps():
    raw_values = [math.exp(-k * k / 8.0) for k in range(-REACH, REACH + 1)]
    total = sum(raw_values)
    return [v / total for v in raw_values]


TAPS = gauss_taps()


def iota(shape, dim):
    return lax.broadcasted_iota(i32, shape, dim)


def eye():
    return iota((128, 128), 0) == iota((128, 128), 1)


def to_row(column):
    same = eye()
    return [
        jnp.sum(jnp.where(same, column[i : i + 128], 0.0), axis=0, keepdims=True)
        for i in range(0, column.shape[0], 128)
    ]


def to_column(row):
    return jnp.sum(jnp.where(eye(), row, 0.0), axis=1, keepdims=True)


def coded(rows):
    top = jnp.maximum(jnp.max(jnp.abs(rows), axis=1, keepdims=True), 1e-30)
    exponent = jnp.ceil(jnp.log2(top)) - 15.0
    q = jnp.floor(rows * jnp.exp2(-exponent) + 0.5)
    q = jnp.clip(q, -32767.0, 32767.0).astype(i32)
    return (q[:, : F // 2] << 16) | (q[:, F // 2 :] & 0xFFFF), exponent


def integers(packed):
    return jnp.concatenate([packed >> 16, (packed << 16) >> 16], axis=1)


def halves(packed):
    q = integers(packed)
    return (q >> 8).astype(f32).astype(bf16), (q & 255).astype(f32).astype(bf16)


def info_rows(*rows):
    row_id = iota((8, 128), 0)
    block = jnp.zeros((8, 128), i32)
    for i, row in enumerate(rows):
        block = jnp.where(row_id == i, row.astype(i32), block)
    return jnp.concatenate([block, jnp.zeros((8, 128), i32)], axis=1)


def kernel(
    cnt, drag_ref, w_ref, own_ref, col_ref, out_ref,
    lhs, dragk, tf, mo, mr, ls, lr, plc, u, xs, xr, hl, rhs, sx, edge, hx, hxr, hz, hzr, hcr, zx, ax,
    m_s, m_r, t_s, t_r, x_s, x_r, hx_s, hx_r, hz_s, hz_r, hc_s, hc_r,
):
    na, nb = lax.axis_size("gx"), lax.axis_size("gz")
    a, b = lax.axis_index("gx"), lax.axis_index("gz")
    a_up, a_dn = lax.rem(a + 1, na), lax.rem(a + na - 1, na)
    b_up, b_dn = lax.rem(b + 1, nb), lax.rem(b + nb - 1, nb)
    odd = lax.rem(b, 2)
    flip = b + 1 - 2 * odd
    b_up2, b_dn2 = lax.rem(b + 2, nb), lax.rem(b + nb - 2, nb)
    relay = jnp.where(odd == 0, b_up2, b_dn2)
    sides_x = ((a_up, b), (a_dn, b))
    sides_z = ((a, b_up), (a, b_dn))
    barrier = pltpu.get_barrier_semaphore()
    for other in sides_x + sides_z + ((a, b_up2), (a, b_dn2)):
        pl.semaphore_signal(barrier, inc=1, device_id=other, device_id_type=MESH)

    def send(src, dst, s_sem, r_sem, to):
        copy = pltpu.make_async_remote_copy(
            src_ref=src, dst_ref=dst, send_sem=s_sem, recv_sem=r_sem,
            device_id=to, device_id_type=MESH,
        )
        copy.start()
        return copy

    gap = iota((NY, NY), 0) - iota((NY, NY), 1)
    band = jnp.zeros((NY, NY), f32)
    for k in range(2 * REACH + 1):
        band = jnp.where(gap == k - REACH, TAPS[k], band)

    def along_y(rows):
        return jnp.dot(rows, band, precision=HIGHEST, preferred_element_type=f32)

    slot = iota((1, P_SIZE), 1)
    drag = drag_ref[...].astype(f32)
    t_id = iota((32, P_SIZE), 0)
    starts, total = [], cnt[0, 0]
    for d in range(4):
        starts.append(total)
        total = total + cnt[0, d + 1]
    for d in range(4):
        rel = slot - starts[d]
        group = jnp.where((rel >= 0) & (rel < cnt[0, d + 1]), rel >> 3, -1)
        mask = group == t_id
        for c in range(CH):
            lhs[d * 128 + c * 32 : d * 128 + c * 32 + 32, :] = jnp.where(
                mask, drag[c : c + 1, :], 0.0
            ).astype(bf16)
    moved = along_y(jnp.dot(lhs[...], w_ref[...], preferred_element_type=f32))
    for d in range(4):
        for c in range(CH):
            tf[d * 32 : d * 32 + 32, c * NY : (c + 1) * NY] = moved[
                d * 128 + c * 32 : d * 128 + c * 32 + 32, :
            ]
    v, e = coded(tf[0:128, :])
    info = info_rows(to_row(e)[0])
    for d in range(4):
        mo[d, 0:32, :] = v[d * 32 : d * 32 + 32, :]
        mo[d, 32:40, :] = info
    pl.semaphore_wait(barrier, 6)
    copies = []
    for d, to in ((2, sides_z[0]), (3, sides_z[1]), (0, sides_x[0]), (1, sides_x[1])):
        copies.append(send(mo.at[d], mr.at[d], m_s.at[d], m_r.at[d], to))
    m_copies = list(copies)

    dragk[...] = jnp.where(slot < cnt[0, 0], drag, 0.0)
    near = (iota((32, 256), 1) >> 3) == iota((32, 256), 0)
    own_codes, own_cols = own_ref[...], col_ref[...]
    list_copies = []

    def ship(i):
        copy = send(ls.at[i], lr.at[0, i], t_s.at[0, i], t_r.at[0, i], (a, flip))
        copies.append(copy)
        list_copies.append(copy)

    for half in range(2):
        for g in range(4 * half, 4 * half + 4):
            part = dragk[:, g * 256 : (g + 1) * 256]
            rows = jnp.concatenate(
                [jnp.where(near, part[c : c + 1, :], 0.0) for c in range(CH)], axis=0
            )
            made = along_y(
                jnp.dot(
                    rows.astype(bf16), w_ref[g * 256 : (g + 1) * 256, :], preferred_element_type=f32
                )
            )
            for c in range(CH):
                tf[g * 32 : g * 32 + 32, c * NY : (c + 1) * NY] = made[c * 32 : c * 32 + 32, :]
        at = half * 128
        v, e = coded(tf[at : at + 128, :])
        ls[half, 0:128, :] = v
        ls[half, 128:136, :] = info_rows(
            own_codes[:, at : at + 128], own_cols[:, at : at + 128], to_row(e)[0]
        )
        ship(half)

    lane = iota((1, 128), 1)
    e_row = jnp.zeros((1, 128), i32)
    for d in (0, 1, 2, 3):
        m_copies[{2: 0, 3: 1, 0: 2, 1: 3}[d]].wait_recv()
        ls[2, d * 32 : d * 32 + 32, :] = mr[d, 0:32, :]
        e_row = jnp.where((lane >> 5) == d, mr[d, 32:33, 0:128], e_row)
    ls[2, 128:136, :] = info_rows(own_codes[:, 256:384], own_cols[:, 256:384], e_row)
    ship(2)

    before = (iota((NT, NT), 0) < iota((NT, NT), 1)).astype(f32).astype(bf16)
    slot_id = iota((KT, NT), 0).astype(f32)
    sub = iota((8, 128), 0)
    sub3 = iota((8, NT), 0)

    def compact(j, chunk, step_z):
        infos = [chunk(i)[128:136, 0:128] for i in range(3)]
        codes = jnp.concatenate([p[0:1] for p in infos], axis=1)
        cols = jnp.concatenate([p[1:2] for p in infos], axis=1)
        exps = jnp.concatenate([p[2:3] for p in infos], axis=1)
        hit = (codes == 3 * sub3 + 1 + step_z) & (sub3 < 3)
        ranks = jnp.dot(hit.astype(f32).astype(bf16), before, preferred_element_type=f32)
        pos = jnp.where(hit, ranks, -1.0)
        for s in range(3):
            plc[s * KT : (s + 1) * KT, :] = (
                (pos[s : s + 1, :] == slot_id).astype(f32).astype(bf16)
            )
        for i in range(3):
            hi, lo = halves(chunk(i)[0:128, :])
            u[i * 128 : (i + 1) * 128, 0:F] = hi
            u[i * 128 : (i + 1) * 128, F : 2 * F] = lo
        fields = jnp.zeros((8, NT), f32)
        for i, row in enumerate((cols >> 5, cols & 31, exps, jnp.ones((1, NT), i32))):
            fields = jnp.where(sub3 == i, row.astype(f32), fields)
        got = lax.dot_general(
            fields.astype(bf16), plc[...], (((1,), (1,)), ((), ())), preferred_element_type=f32
        )
        col_f = got[0:1] * 32.0 + got[1:2] - jnp.where(got[3:4] > 0.5, 0.0, 1.0)
        exp_f = got[2:3]
        for n, s in ((0, 2), (1, 0)):
            out = jnp.dot(
                plc[s * KT : (s + 1) * KT, :], u[...], preferred_element_type=f32
            ).astype(i32)
            q = (out[:, 0:F] << 8) + out[:, F : 2 * F]
            xs[n, j, 0:128, :] = (q[:, : F // 2] << 16) | (q[:, F // 2 :] & 0xFFFF)
            xs[n, j, 128:136, :] = info_rows(
                col_f[:, s * KT : (s + 1) * KT], exp_f[:, s * KT : (s + 1) * KT]
            )
            x_copies[n, j] = send(
                xs.at[n, j], xr.at[n, j], x_s.at[n, j], x_r.at[n, j], sides_x[n]
            )
            copies.append(x_copies[n, j])
        mid = jnp.dot(plc[KT : 2 * KT, :], u[...], preferred_element_type=f32).astype(bf16)
        rhs[0:128, :] = mid[:, 0:F]
        rhs[128:256, :] = mid[:, F : 2 * F]
        one_hot(0, col_f[:, KT : 2 * KT], exp_f[:, KT : 2 * KT])

    x_copies = {}
    row_id = iota((COLS + 256, 128), 0)
    edge_id = row_id - COLS
    edge_col = ((edge_id & 127) >> 2) * CZ + (edge_id & 3) + jnp.where(edge_id >= 128, CZ - REACH, 0)
    row_col = jnp.where(row_id < COLS, row_id, edge_col).astype(f32)

    def one_hot(slot_at, col_f, exp_f):
        scale = jnp.exp2(exp_f)
        h = jnp.where(row_col == col_f, scale, 0.0)
        hl[:, slot_at * 256 : slot_at * 256 + 128] = (h * 256.0).astype(bf16)
        hl[:, slot_at * 256 + 128 : slot_at * 256 + 256] = h.astype(bf16)

    def deposit(j):
        for n in range(2):
            x_copies[n, j].wait_recv()
            at = 256 * (n + 1)
            hi, lo = halves(xr[n, j, 0:128, :])
            rhs[at : at + 128, :] = hi
            rhs[at + 128 : at + 256, :] = lo
            got = xr[n, j, 128:136, 0:128].astype(f32)
            one_hot(n + 1, got[0:1], got[1:2])
        for i in range(5):
            part = jnp.dot(
                hl[i * 256 : (i + 1) * 256, :], rhs[...], preferred_element_type=f32
            )
            if i < 4:
                at = 128 + i * 256
                if j:
                    part = part + sx[at : at + 256, :]
                sx[at : at + 256, :] = part
            else:
                if j:
                    part = part + edge[...]
                edge[...] = part

    toward = jnp.where(odd == 0, -1, 1)
    compact(0, lambda i: ls[i], 0)
    relay_copies = []
    for i in range(3):
        list_copies[i].wait_recv()
        copy = send(lr.at[0, i], lr.at[1, i], t_s.at[1, i], t_r.at[1, i], (a, relay))
        copies.append(copy)
        relay_copies.append(copy)
    deposit(0)
    compact(1, lambda i: lr[0, i], toward)
    deposit(1)
    for i in range(3):
        relay_copies[i].wait_recv()
    compact(2, lambda i: lr[1, i], -toward)
    deposit(2)

    ve, ee = coded(edge[...])
    ee_rows = to_row(ee)
    z_copies = []
    for n, s in ((0, 1), (1, 0)):
        hz[n, 0:128, :] = ve[s * 128 : (s + 1) * 128, :]
        hz[n, 128:136, :] = info_rows(ee_rows[s])
        z_copies.append(send(hz.at[n], hzr.at[n], hz_s.at[n], hz_r.at[n], sides_z[n]))
    h_copies = []
    for n in range(2):
        at = COLS if n == 0 else 128
        vx, ex = coded(sx[at : at + 128, :])
        hx[n, 0:128, :] = vx
        here = 112 if n == 0 else 0
        hx[n, 128:144, :] = ve[here : here + 16, :]
        hx[n, 144:152, :] = info_rows(to_row(ex)[0], ee_rows[0], ee_rows[1])
        hx[n, 152:168, :] = ve[128 + here : 128 + here + 16, :]
        h_copies.append(send(hx.at[n], hxr.at[n], hx_s.at[n], hx_r.at[n], sides_x[n]))
    copies += z_copies + h_copies
    c_copies = []
    for n in range(2):
        h_copies[n].wait_recv()
        for m in range(2):
            at = 144 if m == 0 else 128
            copy = send(
                hxr.at[n, pl.ds(at, 24)], hcr.at[n, m], hc_s.at[n, m], hc_r.at[n, m], sides_z[m]
            )
            c_copies.append(copy)
    copies += c_copies
    for n in range(2):
        got = hxr[n, 0:128, :]
        scale = jnp.exp2(to_column(hxr[n, 144:145, 0:128].astype(f32)))
        at = 0 if n == 0 else COLS + 128
        sx[at : at + 128, :] = integers(got).astype(f32) * scale

    EXT = (CZ + 2 * REACH) * CH

    def x_pass(x, _):
        total = None
        for k in range(2 * REACH + 1):
            at = pl.multiple_of((x + k) * CZ, CZ)
            term = sx[pl.ds(at, CZ), :] * TAPS[k]
            total = term if total is None else total + term
        for c in range(CH):
            ax[pl.ds(x * EXT + 4 * CH + c, CZ, stride=CH), :] = total[:, c * NY : (c + 1) * NY]
        return 0

    lax.fori_loop(0, CX, x_pass, 0)

    for n in range(2):
        z_copies[n].wait_recv()
    for copy in c_copies:
        copy.wait_recv()
    for n in range(2):
        scale = jnp.exp2(to_column(hzr[n, 128:129, 0:128].astype(f32)))
        main = integers(hzr[n, 0:128, :]).astype(f32) * scale
        for c in range(CH):
            zx[n, pl.ds(4 * 4 * CH + c, 128, stride=CH), :] = main[:, c * NY : (c + 1) * NY]
        for m in range(2):
            data_at, info_at = (8, 0) if n == 0 else (0, 16)
            e_corner = hcr[m, n, info_at + (2 if n == 0 else 1) : info_at + (3 if n == 0 else 2), 0:128]
            col = jnp.exp2(to_column(e_corner.astype(f32)))
            here = 112 if m == 0 else 0
            corner = integers(hcr[m, n, data_at : data_at + 16, :]).astype(f32) * col[here : here + 16]
            base = 0 if m == 0 else (CX + REACH) * 4 * CH
            for c in range(CH):
                zx[n, pl.ds(base + c, 16, stride=CH), :] = corner[:, c * NY : (c + 1) * NY]

    def z_pass(x, _):
        for n in range(2):
            total = None
            for k in range(2 * REACH + 1):
                at = pl.multiple_of((x + k) * 4 * CH, 4 * CH)
                term = zx[n, pl.ds(at, 4 * CH), :] * TAPS[k]
                total = term if total is None else total + term
            at = x * EXT + (0 if n == 0 else (CZ + REACH) * CH)
            ax[pl.ds(pl.multiple_of(at, 8), 4 * CH), :] = total
        total = None
        for k in range(2 * REACH + 1):
            term = ax[pl.ds(x * EXT + CH * k, CZ * CH), :] * TAPS[k]
            total = term if total is None else total + term
        out_ref[pl.ds(pl.multiple_of(x * CZ * CH, CZ * CH), CZ * CH), :] = total
        return 0

    lax.fori_loop(0, CX, z_pass, 0)
    for copy in copies:
        copy.wait_send()


def local(particle_drag, particle_weights, migration_counts, tile_owner, tile_column):
    vmem = pl.BlockSpec(memory_space=pltpu.VMEM)
    dma = pltpu.SemaphoreType.DMA
    out = pl.pallas_call(
        kernel,
        out_shape=jax.ShapeDtypeStruct((COLS * CH, NY), f32),
        in_specs=[pl.BlockSpec(memory_space=pltpu.SMEM), vmem, vmem, vmem, vmem],
        out_specs=vmem,
        scratch_shapes=[
            pltpu.VMEM((512, P_SIZE), bf16),
            pltpu.VMEM((CH, P_SIZE), f32),
            pltpu.VMEM((256, F), f32),
            pltpu.VMEM((4, 40, 256), i32),
            pltpu.VMEM((4, 40, 256), i32),
            pltpu.VMEM((3, 136, 256), i32),
            pltpu.VMEM((2, 3, 136, 256), i32),
            pltpu.VMEM((NT, NT), bf16),
            pltpu.VMEM((NT, 2 * F), bf16),
            pltpu.VMEM((2, 3, 136, 256), i32),
            pltpu.VMEM((2, 3, 136, 256), i32),
            pltpu.VMEM((COLS + 256, 768), bf16),
            pltpu.VMEM((768, F), bf16),
            pltpu.VMEM((COLS + 256, F), f32),
            pltpu.VMEM((256, F), f32),
            pltpu.VMEM((2, 168, 256), i32),
            pltpu.VMEM((2, 168, 256), i32),
            pltpu.VMEM((2, 136, 256), i32),
            pltpu.VMEM((2, 136, 256), i32),
            pltpu.VMEM((2, 2, 24, 256), i32),
            pltpu.VMEM((2, 640, NY), f32),
            pltpu.VMEM((CX * (CZ + 2 * REACH) * CH, NY), f32),
            dma((4,)), dma((4,)),
            dma((2, 3)), dma((2, 3)),
            dma((2, 3)), dma((2, 3)),
            dma((2,)), dma((2,)),
            dma((2,)), dma((2,)),
            dma((2, 2)), dma((2, 2)),
        ],
        compiler_params=pltpu.CompilerParams(
            collective_id=0, has_side_effects=True, vmem_limit_bytes=48 * 1024 * 1024
        ),
        cost_estimate=pl.CostEstimate(
            flops=8_000_000_000, bytes_accessed=3_000_000, transcendentals=0
        ),
        name="deposit_and_filter",
    )(
        migration_counts.reshape(1, 5),
        particle_drag.reshape(CH, P_SIZE),
        particle_weights.reshape(P_SIZE, NY),
        tile_owner.reshape(1, NT),
        tile_column.reshape(1, NT),
    )
    return out.reshape(CX, CZ, CH, NY)


def solution(mesh):
    in_specs = (
        P("gx", "gz", None, None),
        P("gx", "gz", None, None),
        P("gx", "gz", None),
        P("gx", "gz", None, None),
        P("gx", "gz", None),
    )
    out_specs = P("gx", "gz", None, None)
    return jax.shard_map(local, mesh=mesh, in_specs=in_specs, out_specs=out_specs, check_vma=False)
```

```python
import math

import jax
import jax.numpy as jnp
from jax import lax
from jax.experimental import pallas as pl
from jax.experimental.pallas import tpu as pltpu
from jax.sharding import PartitionSpec as P

CX = 32
CZ = 32
NY = 128
CH = 4
P_SIZE = 2048
G = 8
REACH = 4
M = 256
KT = 128
NT = 384
F = CH * NY
MOVED_AT = P_SIZE - 4 * M
KEPT = (P_SIZE - M) // G
CHUNKS = ((0, 136), (136, 104), (240, 64), (304, 72))
MOVED_ROW = 240
UNPACKED = (0, 128, 256, 320)
LIST = 376
COLS = CX * CZ
MESH = pl.DeviceIdType.MESH
f32, bf16, i32 = jnp.float32, jnp.bfloat16, jnp.int32
HIGHEST = lax.Precision.HIGHEST


def gauss_taps():
    raw_values = [math.exp(-k * k / 8.0) for k in range(-REACH, REACH + 1)]
    total = sum(raw_values)
    return [v / total for v in raw_values]


TAPS = gauss_taps()


def iota(shape, dim):
    return lax.broadcasted_iota(i32, shape, dim)


def eye():
    return iota((128, 128), 0) == iota((128, 128), 1)


def to_row(column):
    rows = []
    for i in range(0, column.shape[0], 128):
        part = column[i : i + 128]
        shape = (part.shape[0], 128)
        rows.append(
            jnp.sum(jnp.where(iota(shape, 0) == iota(shape, 1), part, 0.0), axis=0, keepdims=True)
        )
    return rows


def to_column(row):
    return jnp.sum(jnp.where(eye(), row, 0.0), axis=1, keepdims=True)


def coded(rows):
    top = jnp.maximum(jnp.max(jnp.abs(rows), axis=1, keepdims=True), 1e-30)
    exponent = jnp.ceil(jnp.log2(top)) - 15.0
    q = jnp.floor(rows * jnp.exp2(-exponent) + 0.5)
    q = jnp.clip(q, -32767.0, 32767.0).astype(i32)
    return (q[:, : F // 2] << 16) | (q[:, F // 2 :] & 0xFFFF), exponent


def integers(packed):
    return jnp.concatenate([packed >> 16, (packed << 16) >> 16], axis=1)


def halves(packed):
    q = integers(packed)
    return (q >> 8).astype(f32).astype(bf16), (q & 255).astype(f32).astype(bf16)


def info_rows(*rows):
    row_id = iota((8, 128), 0)
    block = jnp.zeros((8, 128), i32)
    for i, row in enumerate(rows):
        block = jnp.where(row_id == i, row.astype(i32), block)
    return jnp.concatenate([block, jnp.zeros((8, 128), i32)], axis=1)


def kernel(
    cnt_hbm, drag_hbm, w_hbm, own_hbm, col_hbm, out_ref,
    cnt, drag_ref, w_ref, own_ref, col_ref,
    lhs, dragk, tf, mo, mr, ls, lr, plc, u, xs, xr, rhs, sx, edge, hx, hxr, hz, hzr, ho, hor, hc, hcr, part_x, zx, ax,
    in_s, m_s, m_r, t_s, t_r, x_s, x_r, hx_s, hx_r, hz_s, hz_r, ho_s, ho_r, hc_s, hc_r,
):
    na, nb = lax.axis_size("gx"), lax.axis_size("gz")
    a, b = lax.axis_index("gx"), lax.axis_index("gz")
    a_up, a_dn = lax.rem(a + 1, na), lax.rem(a + na - 1, na)
    b_up, b_dn = lax.rem(b + 1, nb), lax.rem(b + nb - 1, nb)
    odd = lax.rem(b, 2)
    flip = b + 1 - 2 * odd
    b_up2, b_dn2 = lax.rem(b + 2, nb), lax.rem(b + nb - 2, nb)
    relay = jnp.where(odd == 0, b_up2, b_dn2)
    sides_x = ((a_up, b), (a_dn, b))
    sides_z = ((a, b_up), (a, b_dn))
    barrier = pltpu.get_barrier_semaphore()
    for other in sides_x + sides_z + ((a, b_up2), (a, b_dn2)):
        pl.semaphore_signal(barrier, inc=1, device_id=other, device_id_type=MESH)
    fetches = []
    for i, (src, dst) in enumerate(
        ((cnt_hbm, cnt), (drag_hbm, drag_ref), (w_hbm, w_ref), (own_hbm, own_ref), (col_hbm, col_ref))
    ):
        fetch = pltpu.make_async_copy(src, dst, in_s.at[i])
        fetch.start()
        fetches.append(fetch)

    def send(src, dst, s_sem, r_sem, to):
        copy = pltpu.make_async_remote_copy(
            src_ref=src, dst_ref=dst, send_sem=s_sem, recv_sem=r_sem,
            device_id=to, device_id_type=MESH,
        )
        copy.start()
        return copy

    gap = iota((NY, NY), 0) - iota((NY, NY), 1)
    band = jnp.zeros((NY, NY), f32)
    for k in range(2 * REACH + 1):
        band = jnp.where(gap == k - REACH, TAPS[k], band)

    def along_y(rows):
        return jnp.dot(rows, band, precision=HIGHEST, preferred_element_type=f32)

    for fetch in fetches[:2]:
        fetch.wait()
    slot = iota((1, P_SIZE), 1)
    drag = drag_ref[...].astype(f32)
    late, late_drag = slot[:, MOVED_AT:], drag[:, MOVED_AT:]
    t_id = iota((32, P_SIZE - MOVED_AT), 0)
    start = cnt[0, 0]
    for d in range(4):
        rel = late - start
        group = jnp.where((rel >= 0) & (rel < cnt[0, d + 1]), rel >> 3, -1)
        start = start + cnt[0, d + 1]
        mask = group == t_id
        for c in range(CH):
            lhs[d * 128 + c * 32 : d * 128 + c * 32 + 32, :] = jnp.where(
                mask, late_drag[c : c + 1, :], 0.0
            ).astype(bf16)
    fetches[2].wait()
    moved = along_y(
        jnp.dot(lhs[...], w_ref[MOVED_AT:P_SIZE, :], preferred_element_type=f32)
    )
    for d in range(4):
        for c in range(CH):
            tf[d * 32 : d * 32 + 32, c * NY : (c + 1) * NY] = moved[
                d * 128 + c * 32 : d * 128 + c * 32 + 32, :
            ]
    v, e = coded(tf[0:128, :])
    info = info_rows(to_row(e)[0])
    for d in range(4):
        mo[d, 0:32, :] = v[d * 32 : d * 32 + 32, :]
        mo[d, 32:40, :] = info
    dragk[...] = jnp.where(slot < cnt[0, 0], drag, 0.0)
    near = (iota((32, 256), 1) >> 3) == iota((32, 256), 0)
    copies, list_copies, m_copies = [], [], {}

    def ship(i):
        at, size = CHUNKS[i]
        copy = send(
            ls.at[pl.ds(at, size)], lr.at[0, pl.ds(at, size)], t_s.at[0, i], t_r.at[0, i], (a, flip)
        )
        copies.append(copy)
        list_copies.append(copy)

    for fetch in fetches[3:]:
        fetch.wait()
    own_codes, own_cols = own_ref[...], col_ref[...]
    for half, groups in ((0, range(0, 4)), (1, range(4, 7))):
        for g in groups:
            part = dragk[:, g * 256 : (g + 1) * 256]
            rows = jnp.concatenate(
                [jnp.where(near, part[c : c + 1, :], 0.0) for c in range(CH)], axis=0
            )
            made = along_y(
                jnp.dot(
                    rows.astype(bf16), w_ref[g * 256 : (g + 1) * 256, :], preferred_element_type=f32
                )
            )
            for c in range(CH):
                tf[g * 32 : g * 32 + 32, c * NY : (c + 1) * NY] = made[c * 32 : c * 32 + 32, :]
        if half:
            tf[KEPT:256, :] = jnp.zeros((256 - KEPT, F), f32)
        v, e = coded(tf[half * 128 : half * 128 + 128, :])
        at, size = CHUNKS[half]
        ls[at : at + size - 8, :] = v[0 : size - 8, :]
        if half:
            info = info_rows(to_row(e)[0])
        else:
            info = info_rows(
                to_row(e)[0], *(r[:, i : i + 128] for r in (own_codes, own_cols) for i in (0, 128, 256))
            )
        ls[at + size - 8 : at + size, :] = info
        if not half:
            pl.semaphore_wait(barrier, 6)
        ship(half)
        if not half:
            for d, to in ((2, sides_z[0]), (3, sides_z[1]), (0, sides_x[0]), (1, sides_x[1])):
                m_copies[d] = send(mo.at[d], mr.at[d], m_s.at[d], m_r.at[d], to)
                copies.append(m_copies[d])

    lane = iota((1, 128), 1)
    e_row = jnp.zeros((1, 128), i32)
    for d in (0, 1, 2, 3):
        m_copies[d].wait_recv()
        at = MOVED_ROW + d * 32
        ls[at : at + 32, :] = mr[d, 0:32, :]
        e_row = jnp.where((lane >> 5) == d, mr[d, 32:33, 0:128], e_row)
        if d == 1:
            ship(2)
    ls[MOVED_ROW + 128 : MOVED_ROW + 136, :] = info_rows(e_row)
    ship(3)

    before = (iota((NT, NT), 0) < iota((NT, NT), 1)).astype(f32).astype(bf16)
    slot_id = iota((KT, NT), 0).astype(f32)
    sub3 = iota((8, NT), 0)
    lane3 = iota((8, NT), 1)
    u[:, KEPT:256, :] = jnp.zeros((3, 256 - KEPT, 2 * F), bf16)

    def unpack(j, part, i):
        at, size = CHUNKS[i]
        rows = size if i == 2 else size - 8
        hi, lo = halves(part[at : at + rows, :])
        to = UNPACKED[i]
        u[j, to : to + rows, 0:F] = hi
        u[j, to : to + rows, F : 2 * F] = lo

    def placing(j, part, step_z):
        info = part[128:136, 0:128]
        codes = jnp.concatenate([info[1:2], info[2:3], info[3:4]], axis=1)
        live = (sub3 < 3) & ((lane3 < KEPT) | (lane3 >= 256))
        hit = (codes == 3 * sub3 + 1 + step_z) & live
        ranks = jnp.dot(hit.astype(f32).astype(bf16), before, preferred_element_type=f32)
        pos = jnp.where(hit, ranks, -1.0)
        for s in range(3):
            plc[j, s * KT : (s + 1) * KT, :] = (
                (pos[s : s + 1, :] == slot_id).astype(f32).astype(bf16)
            )

    x_copies = {}

    def compact(j, part):
        infos = [part[at + size - 8 : at + size, 0:128] for at, size in CHUNKS]
        cols = jnp.concatenate([infos[0][4:5], infos[0][5:6], infos[0][6:7]], axis=1)
        exps = jnp.concatenate([infos[0][0:1], infos[1][0:1], infos[3][0:1]], axis=1)
        fields = jnp.zeros((8, NT), f32)
        for i, row in enumerate((cols >> 5, cols & 31, exps, jnp.ones((1, NT), i32))):
            fields = jnp.where(sub3 == i, row.astype(f32), fields)
        got = lax.dot_general(
            fields.astype(bf16), plc[j], (((1,), (1,)), ((), ())), preferred_element_type=f32
        )
        col_f = got[0:1] * 32.0 + got[1:2] - jnp.where(got[3:4] > 0.5, 0.0, 1.0)
        exp_f = got[2:3]
        for n, s in ((0, 2), (1, 0)):
            out = jnp.dot(
                plc[j, s * KT : (s + 1) * KT, :], u[j], preferred_element_type=f32
            ).astype(i32)
            q = (out[:, 0:F] << 8) + out[:, F : 2 * F]
            xs[n, j, 0:128, :] = (q[:, : F // 2] << 16) | (q[:, F // 2 :] & 0xFFFF)
            xs[n, j, 128:136, :] = info_rows(
                col_f[:, s * KT : (s + 1) * KT], exp_f[:, s * KT : (s + 1) * KT]
            )
            x_copies[n, j] = send(
                xs.at[n, j], xr.at[n, j], x_s.at[n, j], x_r.at[n, j], sides_x[n]
            )
            copies.append(x_copies[n, j])
        mid = jnp.dot(plc[j, KT : 2 * KT, :], u[j], preferred_element_type=f32).astype(bf16)
        rhs[j, 0:128, :] = mid[:, 0:F]
        rhs[j, 128:256, :] = mid[:, F : 2 * F]
        return col_f[:, KT : 2 * KT], jnp.exp2(exp_f[:, KT : 2 * KT])

    def one_hot(i, spots):
        row_id = iota((256, 128), 0)
        if i < 4:
            row_col = row_id + 256 * i
        else:
            row_col = ((row_id & 127) >> 2) * CZ + (row_id & 3)
            row_col = row_col + jnp.where(row_id >= 128, CZ - REACH, 0)
        row_col = row_col.astype(f32)
        parts = []
        for col_f, scale in spots:
            h = jnp.where(row_col == col_f, scale, 0.0)
            parts += [(h * 256.0).astype(bf16), h.astype(bf16)]
        return jnp.concatenate(parts, axis=1)

    def arrived(j, spot):
        spots = [spot]
        for n in range(2):
            x_copies[n, j].wait_recv()
            at = 256 * (n + 1)
            hi, lo = halves(xr[n, j, 0:128, :])
            rhs[j, at : at + 128, :] = hi
            rhs[j, at + 128 : at + 256, :] = lo
            got = xr[n, j, 128:136, 0:128].astype(f32)
            spots.append((got[0:1], jnp.exp2(got[1:2])))
        return spots

    def deposit(j, i, spots):
        part = jnp.dot(one_hot(i, spots), rhs[j], preferred_element_type=f32)
        if i < 4:
            at = 128 + i * 256
            if j:
                part = part + sx[at : at + 256, :]
            sx[at : at + 256, :] = part
        else:
            if j:
                part = part + edge[...]
            edge[...] = part

    toward = jnp.where(odd == 0, -1, 1)
    placing(0, ls, 0)
    for i in range(4):
        unpack(0, ls, i)
    relay_copies = []

    def pass_on(i):
        at, size = CHUNKS[i]
        list_copies[i].wait_recv()
        copy = send(
            lr.at[0, pl.ds(at, size)], lr.at[1, pl.ds(at, size)], t_s.at[1, i], t_r.at[1, i], (a, relay)
        )
        copies.append(copy)
        relay_copies.append(copy)

    pass_on(0)
    spot = compact(0, ls)
    placing(1, lr.at[0], toward)
    unpack(1, lr.at[0], 0)
    for i in range(1, 4):
        pass_on(i)
        unpack(1, lr.at[0], i)
    next_spot = compact(1, lr.at[0])
    spots = arrived(0, spot)
    for i in range(5):
        deposit(0, i, spots)
    relay_copies[0].wait_recv()
    placing(2, lr.at[1], -toward)
    unpack(2, lr.at[1], 0)
    for i in range(1, 4):
        relay_copies[i].wait_recv()
        unpack(2, lr.at[1], i)
    last_spot = compact(2, lr.at[1])
    spots = arrived(1, next_spot)
    for i in range(5):
        deposit(1, i, spots)
    spots = arrived(2, last_spot)

    deposit(2, 4, spots)
    z_copies, h_copies, c_copies, o_copies = [], [], [], []
    vc, ec = coded(
        jnp.concatenate(
            [edge[at : at + 16, :] for at in (112, 128 + 112, 0, 128)], axis=0
        )
    )
    info = info_rows(to_row(ec)[0])
    for n in range(2):
        hc[n, 0:32, :] = vc[n * 32 : n * 32 + 32, :]
        hc[n, 32:40, :] = info
        c_copies.append(send(hc.at[n], hcr.at[n], hc_s.at[n], hc_r.at[n], sides_x[n]))

    def banded(shape, out_pos, in_pos):
        apart = in_pos - out_pos
        matrix = jnp.zeros(shape, f32)
        for k in range(2 * REACH + 1):
            matrix = jnp.where(apart == 4 * (k - REACH), TAPS[k], matrix)
        return matrix

    own_x = banded((128, 128), iota((128, 128), 0), iota((128, 128), 1))
    for n, s in ((0, 1), (1, 0)):
        made = jnp.dot(
            own_x, edge[s * 128 : (s + 1) * 128, :], precision=HIGHEST, preferred_element_type=f32
        )
        part_x[s, 0:16, :] = made[0:16, :]
        part_x[s, 16:32, :] = made[112:128, :]
        ve, ee = coded(made[16:112, :])
        hz[n, 0:96, :] = ve
        hz[n, 96:104, :] = info_rows(to_row(ee)[0])
        z_copies.append(send(hz.at[n], hzr.at[n], hz_s.at[n], hz_r.at[n], sides_z[n]))
    for n, i in ((0, 3), (1, 0)):
        deposit(2, i, spots)
        at = COLS if n == 0 else 128
        vx, ex = coded(sx[at : at + 128, :])
        hx[n, 0:128, :] = vx
        hx[n, 128:136, :] = info_rows(to_row(ex)[0])
        h_copies.append(send(hx.at[n], hxr.at[n], hx_s.at[n], hx_r.at[n], sides_x[n]))
    i_out, i_in = iota((32, 32), 0), iota((32, 32), 1)
    far_x = banded(
        (32, 32), jnp.where(i_out < 16, i_out, i_out + 96), jnp.where(i_in < 16, i_in - 16, i_in + 112)
    )
    beyond = []
    for n in range(2):
        c_copies[n].wait_recv()
        scale = jnp.exp2(to_column(hcr[n, 32:33, 0:128].astype(f32)))
        beyond.append(integers(hcr[n, 0:32, :]).astype(f32) * scale[n * 32 : n * 32 + 32])
    outer = []
    for s in range(2):
        rows = jnp.concatenate([v[s * 16 : s * 16 + 16] for v in beyond], axis=0)
        outer.append(
            part_x[s] + jnp.dot(far_x, rows, precision=HIGHEST, preferred_element_type=f32)
        )
    vo, eo = coded(jnp.concatenate(outer, axis=0))
    info = info_rows(to_row(eo)[0])
    for n, s in ((0, 1), (1, 0)):
        ho[n, 0:32, :] = vo[s * 32 : s * 32 + 32, :]
        ho[n, 32:40, :] = info
        o_copies.append(send(ho.at[n], hor.at[n], ho_s.at[n], ho_r.at[n], sides_z[n]))
    copies += z_copies + h_copies + c_copies + o_copies
    deposit(2, 1, spots)
    deposit(2, 2, spots)
    for n in range(2):
        h_copies[n].wait_recv()
    for n in range(2):
        got = hxr[n, 0:128, :]
        scale = jnp.exp2(to_column(hxr[n, 128:129, 0:128].astype(f32)))
        at = 0 if n == 0 else COLS + 128
        sx[at : at + 128, :] = integers(got).astype(f32) * scale

    def taps(term):
        total = term(REACH) * TAPS[REACH]
        for k in range(1, REACH + 1):
            total = total + (term(REACH - k) + term(REACH + k)) * TAPS[REACH + k]
        return total

    EXT = (CZ + 2 * REACH) * CH

    def x_pass(x, _):
        total = taps(lambda k: sx[pl.ds(pl.multiple_of((x + k) * CZ, CZ), CZ), :])
        for c in range(CH):
            ax[pl.ds(x * EXT + 4 * CH + c, CZ, stride=CH), :] = total[:, c * NY : (c + 1) * NY]
        inner = taps(lambda k: ax[pl.ds(x * EXT + 4 * CH + CH * k, (CZ - 8) * CH), :])
        at = pl.multiple_of(x * CZ * CH + 4 * CH, 16)
        out_ref[pl.ds(at, (CZ - 8) * CH), :] = inner
        return 0

    lax.fori_loop(0, CX, x_pass, 0)

    for n in range(2):
        z_copies[n].wait_recv()
        scale = jnp.exp2(to_column(hzr[n, 96:97, 0:128].astype(f32)))
        rows = integers(hzr[n, 0:96, :]).astype(f32) * scale[0:96]
        for c in range(CH):
            zx[n, pl.ds(16 * CH + c, 96, stride=CH), :] = rows[:, c * NY : (c + 1) * NY]
    for n in range(2):
        o_copies[n].wait_recv()
        scale = jnp.exp2(to_column(hor[n, 32:33, 0:128].astype(f32)))
        s = 1 - n
        rows = integers(hor[n, 0:32, :]).astype(f32) * scale[s * 32 : s * 32 + 32]
        for half in range(2):
            for c in range(CH):
                zx[n, pl.ds(half * 112 * CH + c, 16, stride=CH), :] = rows[
                    half * 16 : half * 16 + 16, c * NY : (c + 1) * NY
                ]

    W = 4 * CH

    def z_pass(step, _):
        for part in range(4):
            x = step * 4 + part
            for n in range(2):
                at = x * EXT + (0 if n == 0 else (CZ + REACH) * CH)
                ax[pl.ds(pl.multiple_of(at, 8), W), :] = zx[n, pl.ds(pl.multiple_of(x * W, W), W), :]
        for part in range(4):
            x = step * 4 + part
            for z in (0, CZ - REACH):
                total = taps(lambda k: ax[pl.ds(x * EXT + CH * (z + k), W), :])
                out_ref[pl.ds(pl.multiple_of(x * CZ * CH + z * CH, W), W), :] = total
        return 0

    lax.fori_loop(0, CX // 4, z_pass, 0)
    for copy in copies:
        copy.wait_send()


def local(particle_drag, particle_weights, migration_counts, tile_owner, tile_column):
    vmem = pl.BlockSpec(memory_space=pltpu.VMEM)
    dma = pltpu.SemaphoreType.DMA
    hbm = pl.BlockSpec(memory_space=pltpu.HBM)
    out = pl.pallas_call(
        kernel,
        out_shape=jax.ShapeDtypeStruct((COLS * CH, NY), f32),
        in_specs=[hbm] * 5,
        out_specs=vmem,
        scratch_shapes=[
            pltpu.SMEM((1, 5), i32),
            pltpu.VMEM((CH, P_SIZE), bf16),
            pltpu.VMEM((P_SIZE, NY), bf16),
            pltpu.VMEM((1, NT), i32),
            pltpu.VMEM((1, NT), i32),
            pltpu.VMEM((512, P_SIZE - MOVED_AT), bf16),
            pltpu.VMEM((CH, P_SIZE), f32),
            pltpu.VMEM((256, F), f32),
            pltpu.VMEM((4, 40, 256), i32),
            pltpu.VMEM((4, 40, 256), i32),
            pltpu.VMEM((LIST, 256), i32),
            pltpu.VMEM((2, LIST, 256), i32),
            pltpu.VMEM((3, NT, NT), bf16),
            pltpu.VMEM((3, NT, 2 * F), bf16),
            pltpu.VMEM((2, 3, 136, 256), i32),
            pltpu.VMEM((2, 3, 136, 256), i32),
            pltpu.VMEM((3, 768, F), bf16),
            pltpu.VMEM((COLS + 256, F), f32),
            pltpu.VMEM((256, F), f32),
            pltpu.VMEM((2, 136, 256), i32),
            pltpu.VMEM((2, 136, 256), i32),
            pltpu.VMEM((2, 104, 256), i32),
            pltpu.VMEM((2, 104, 256), i32),
            pltpu.VMEM((2, 40, 256), i32),
            pltpu.VMEM((2, 40, 256), i32),
            pltpu.VMEM((2, 40, 256), i32),
            pltpu.VMEM((2, 40, 256), i32),
            pltpu.VMEM((2, 32, F), f32),
            pltpu.VMEM((2, 512, NY), f32),
            pltpu.VMEM((CX * (CZ + 2 * REACH) * CH, NY), f32),
            dma((5,)),
            dma((4,)), dma((4,)),
            dma((2, 4)), dma((2, 4)),
            dma((2, 3)), dma((2, 3)),
            dma((2,)), dma((2,)),
            dma((2,)), dma((2,)),
            dma((2,)), dma((2,)),
            dma((2,)), dma((2,)),
        ],
        compiler_params=pltpu.CompilerParams(
            collective_id=0, has_side_effects=True, vmem_limit_bytes=48 * 1024 * 1024
        ),
        cost_estimate=pl.CostEstimate(
            flops=8_000_000_000, bytes_accessed=3_000_000, transcendentals=0
        ),
        name="deposit_and_filter",
    )(
        migration_counts.reshape(1, 5),
        particle_drag.reshape(CH, P_SIZE),
        particle_weights.reshape(P_SIZE, NY),
        tile_owner.reshape(1, NT),
        tile_column.reshape(1, NT),
    )
    return out.reshape(CX, CZ, CH, NY)


def solution(mesh):
    in_specs = (
        P("gx", "gz", None, None),
        P("gx", "gz", None, None),
        P("gx", "gz", None),
        P("gx", "gz", None, None),
        P("gx", "gz", None),
    )
    out_specs = P("gx", "gz", None, None)
    return jax.shard_map(local, mesh=mesh, in_specs=in_specs, out_specs=out_specs, check_vma=False)
```

```python
import math

import jax
import jax.numpy as jnp
from jax import lax
from jax.experimental import pallas as pl
from jax.experimental.pallas import tpu as pltpu
from jax.sharding import PartitionSpec as P

CX = 32
CZ = 32
NY = 128
CH = 4
P_SIZE = 2048
G = 8
REACH = 4
M = 256
KT = 128
NT = 384
F = CH * NY
MOVED_AT = P_SIZE - 4 * M
KEPT = (P_SIZE - M) // G
CHUNKS = ((0, 136), (136, 104), (240, 64), (304, 72))
MOVED_ROW = 240
UNPACKED = (0, 128, 256, 320)
LIST = 376
COLS = CX * CZ
MESH = pl.DeviceIdType.MESH
f32, bf16, i32 = jnp.float32, jnp.bfloat16, jnp.int32
HIGHEST = lax.Precision.HIGHEST


def gauss_taps():
    raw_values = [math.exp(-k * k / 8.0) for k in range(-REACH, REACH + 1)]
    total = sum(raw_values)
    return [v / total for v in raw_values]


TAPS = gauss_taps()


def iota(shape, dim):
    return lax.broadcasted_iota(i32, shape, dim)


def eye():
    return iota((128, 128), 0) == iota((128, 128), 1)


def to_row(column):
    rows = []
    for i in range(0, column.shape[0], 128):
        part = column[i : i + 128]
        shape = (part.shape[0], 128)
        rows.append(
            jnp.sum(jnp.where(iota(shape, 0) == iota(shape, 1), part, 0.0), axis=0, keepdims=True)
        )
    return rows


def to_column(row):
    return jnp.sum(jnp.where(eye(), row, 0.0), axis=1, keepdims=True)


def coded(rows):
    top = jnp.maximum(jnp.max(jnp.abs(rows), axis=1, keepdims=True), 1e-30)
    exponent = jnp.ceil(jnp.log2(top)) - 15.0
    q = jnp.floor(rows * jnp.exp2(-exponent) + 0.5)
    q = jnp.clip(q, -32767.0, 32767.0).astype(i32)
    return (q[:, : F // 2] << 16) | (q[:, F // 2 :] & 0xFFFF), exponent


def integers(packed):
    return jnp.concatenate([packed >> 16, (packed << 16) >> 16], axis=1)


def halves(packed):
    q = integers(packed)
    return (q >> 8).astype(f32).astype(bf16), (q & 255).astype(f32).astype(bf16)


def info_rows(*rows):
    row_id = iota((8, 128), 0)
    block = jnp.zeros((8, 128), i32)
    for i, row in enumerate(rows):
        block = jnp.where(row_id == i, row.astype(i32), block)
    return jnp.concatenate([block, jnp.zeros((8, 128), i32)], axis=1)


def kernel(
    cnt_hbm, drag_hbm, w_hbm, own_hbm, col_hbm, out_hbm,
    cnt, drag_ref, w_ref, own_ref, col_ref,
    lhs, dragk, tf, mo, mr, ls, lr, plc, u, xs, xr, rhs, sx, edge, hx, hxr, hz, hzr, ho, hor, hc, hcr, part_x, zx, ax, out_ref,
    in_s, out_s, m_s, m_r, t_s, t_r, x_s, x_r, hx_s, hx_r, hz_s, hz_r, ho_s, ho_r, hc_s, hc_r,
):
    na, nb = lax.axis_size("gx"), lax.axis_size("gz")
    a, b = lax.axis_index("gx"), lax.axis_index("gz")
    a_up, a_dn = lax.rem(a + 1, na), lax.rem(a + na - 1, na)
    b_up, b_dn = lax.rem(b + 1, nb), lax.rem(b + nb - 1, nb)
    odd = lax.rem(b, 2)
    flip = b + 1 - 2 * odd
    b_up2, b_dn2 = lax.rem(b + 2, nb), lax.rem(b + nb - 2, nb)
    relay = jnp.where(odd == 0, b_up2, b_dn2)
    sides_x = ((a_up, b), (a_dn, b))
    sides_z = ((a, b_up), (a, b_dn))
    barrier = pltpu.get_barrier_semaphore()
    for other in sides_x + sides_z + ((a, b_up2), (a, b_dn2)):
        pl.semaphore_signal(barrier, inc=1, device_id=other, device_id_type=MESH)
    fetches = []
    for i, (src, dst) in enumerate(
        ((cnt_hbm, cnt), (drag_hbm, drag_ref), (w_hbm, w_ref), (own_hbm, own_ref), (col_hbm, col_ref))
    ):
        fetch = pltpu.make_async_copy(src, dst, in_s.at[i])
        fetch.start()
        fetches.append(fetch)

    def send(src, dst, s_sem, r_sem, to):
        copy = pltpu.make_async_remote_copy(
            src_ref=src, dst_ref=dst, send_sem=s_sem, recv_sem=r_sem,
            device_id=to, device_id_type=MESH,
        )
        copy.start()
        return copy

    gap = iota((NY, NY), 0) - iota((NY, NY), 1)
    band = jnp.zeros((NY, NY), f32)
    for k in range(2 * REACH + 1):
        band = jnp.where(gap == k - REACH, TAPS[k], band)

    def along_y(rows):
        return jnp.dot(rows, band, precision=HIGHEST, preferred_element_type=f32)

    for fetch in fetches[:2]:
        fetch.wait()
    slot = iota((1, P_SIZE), 1)
    drag = drag_ref[...].astype(f32)
    late, late_drag = slot[:, MOVED_AT:], drag[:, MOVED_AT:]
    t_id = iota((32, P_SIZE - MOVED_AT), 0)
    start = cnt[0, 0]
    for d in range(4):
        rel = late - start
        group = jnp.where((rel >= 0) & (rel < cnt[0, d + 1]), rel >> 3, -1)
        start = start + cnt[0, d + 1]
        mask = group == t_id
        for c in range(CH):
            lhs[d * 128 + c * 32 : d * 128 + c * 32 + 32, :] = jnp.where(
                mask, late_drag[c : c + 1, :], 0.0
            ).astype(bf16)
    fetches[2].wait()
    moved = along_y(
        jnp.dot(lhs[...], w_ref[MOVED_AT:P_SIZE, :], preferred_element_type=f32)
    )
    for d in range(4):
        for c in range(CH):
            tf[d * 32 : d * 32 + 32, c * NY : (c + 1) * NY] = moved[
                d * 128 + c * 32 : d * 128 + c * 32 + 32, :
            ]
    v, e = coded(tf[0:128, :])
    info = info_rows(to_row(e)[0])
    for d in range(4):
        mo[d, 0:32, :] = v[d * 32 : d * 32 + 32, :]
        mo[d, 32:40, :] = info
    dragk[...] = jnp.where(slot < cnt[0, 0], drag, 0.0)
    near = (iota((32, 256), 1) >> 3) == iota((32, 256), 0)
    copies, list_copies, m_copies = [], [], {}

    def ship(i):
        at, size = CHUNKS[i]
        copy = send(
            ls.at[pl.ds(at, size)], lr.at[0, pl.ds(at, size)], t_s.at[0, i], t_r.at[0, i], (a, flip)
        )
        copies.append(copy)
        list_copies.append(copy)

    for fetch in fetches[3:]:
        fetch.wait()
    own_codes, own_cols = own_ref[...], col_ref[...]
    for half, groups in ((0, range(0, 4)), (1, range(4, 7))):
        for g in groups:
            part = dragk[:, g * 256 : (g + 1) * 256]
            rows = jnp.concatenate(
                [jnp.where(near, part[c : c + 1, :], 0.0) for c in range(CH)], axis=0
            )
            made = along_y(
                jnp.dot(
                    rows.astype(bf16), w_ref[g * 256 : (g + 1) * 256, :], preferred_element_type=f32
                )
            )
            for c in range(CH):
                tf[g * 32 : g * 32 + 32, c * NY : (c + 1) * NY] = made[c * 32 : c * 32 + 32, :]
        if half:
            tf[KEPT:256, :] = jnp.zeros((256 - KEPT, F), f32)
        v, e = coded(tf[half * 128 : half * 128 + 128, :])
        at, size = CHUNKS[half]
        ls[at : at + size - 8, :] = v[0 : size - 8, :]
        if half:
            info = info_rows(to_row(e)[0])
        else:
            info = info_rows(
                to_row(e)[0], *(r[:, i : i + 128] for r in (own_codes, own_cols) for i in (0, 128, 256))
            )
        ls[at + size - 8 : at + size, :] = info
        if not half:
            pl.semaphore_wait(barrier, 6)
        ship(half)
        if not half:
            for d, to in ((2, sides_z[0]), (3, sides_z[1]), (0, sides_x[0]), (1, sides_x[1])):
                m_copies[d] = send(mo.at[d], mr.at[d], m_s.at[d], m_r.at[d], to)
                copies.append(m_copies[d])

    lane = iota((1, 128), 1)
    e_row = jnp.zeros((1, 128), i32)
    for d in (0, 1, 2, 3):
        m_copies[d].wait_recv()
        at = MOVED_ROW + d * 32
        ls[at : at + 32, :] = mr[d, 0:32, :]
        e_row = jnp.where((lane >> 5) == d, mr[d, 32:33, 0:128], e_row)
        if d == 1:
            ship(2)
    ls[MOVED_ROW + 128 : MOVED_ROW + 136, :] = info_rows(e_row)
    ship(3)

    before = (iota((NT, NT), 0) < iota((NT, NT), 1)).astype(f32).astype(bf16)
    slot_id = iota((KT, NT), 0).astype(f32)
    sub3 = iota((8, NT), 0)
    lane3 = iota((8, NT), 1)
    u[:, KEPT:256, :] = jnp.zeros((3, 256 - KEPT, 2 * F), bf16)

    def unpack(j, part, i):
        at, size = CHUNKS[i]
        rows = size if i == 2 else size - 8
        hi, lo = halves(part[at : at + rows, :])
        to = UNPACKED[i]
        u[j, to : to + rows, 0:F] = hi
        u[j, to : to + rows, F : 2 * F] = lo

    def placing(j, part, step_z):
        info = part[128:136, 0:128]
        codes = jnp.concatenate([info[1:2], info[2:3], info[3:4]], axis=1)
        live = (sub3 < 3) & ((lane3 < KEPT) | (lane3 >= 256))
        hit = (codes == 3 * sub3 + 1 + step_z) & live
        ranks = jnp.dot(hit.astype(f32).astype(bf16), before, preferred_element_type=f32)
        pos = jnp.where(hit, ranks, -1.0)
        for s in range(3):
            plc[j, s * KT : (s + 1) * KT, :] = (
                (pos[s : s + 1, :] == slot_id).astype(f32).astype(bf16)
            )

    x_copies = {}

    def compact(j, part):
        infos = [part[at + size - 8 : at + size, 0:128] for at, size in CHUNKS]
        cols = jnp.concatenate([infos[0][4:5], infos[0][5:6], infos[0][6:7]], axis=1)
        exps = jnp.concatenate([infos[0][0:1], infos[1][0:1], infos[3][0:1]], axis=1)
        fields = jnp.zeros((8, NT), f32)
        for i, row in enumerate((cols >> 5, cols & 31, exps, jnp.ones((1, NT), i32))):
            fields = jnp.where(sub3 == i, row.astype(f32), fields)
        got = lax.dot_general(
            fields.astype(bf16), plc[j], (((1,), (1,)), ((), ())), preferred_element_type=f32
        )
        col_f = got[0:1] * 32.0 + got[1:2] - jnp.where(got[3:4] > 0.5, 0.0, 1.0)
        exp_f = got[2:3]
        for n, s in ((0, 2), (1, 0)):
            out = jnp.dot(
                plc[j, s * KT : (s + 1) * KT, :], u[j], preferred_element_type=f32
            ).astype(i32)
            q = (out[:, 0:F] << 8) + out[:, F : 2 * F]
            xs[n, j, 0:128, :] = (q[:, : F // 2] << 16) | (q[:, F // 2 :] & 0xFFFF)
            xs[n, j, 128:136, :] = info_rows(
                col_f[:, s * KT : (s + 1) * KT], exp_f[:, s * KT : (s + 1) * KT]
            )
            x_copies[n, j] = send(
                xs.at[n, j], xr.at[n, j], x_s.at[n, j], x_r.at[n, j], sides_x[n]
            )
            copies.append(x_copies[n, j])
        mid = jnp.dot(plc[j, KT : 2 * KT, :], u[j], preferred_element_type=f32).astype(bf16)
        rhs[j, 0:128, :] = mid[:, 0:F]
        rhs[j, 128:256, :] = mid[:, F : 2 * F]
        return col_f[:, KT : 2 * KT], jnp.exp2(exp_f[:, KT : 2 * KT])

    def one_hot(i, spots):
        row_id = iota((256, 128), 0)
        if i < 4:
            row_col = row_id + 256 * i
        else:
            row_col = ((row_id & 127) >> 2) * CZ + (row_id & 3)
            row_col = row_col + jnp.where(row_id >= 128, CZ - REACH, 0)
        row_col = row_col.astype(f32)
        parts = []
        for col_f, scale in spots:
            h = jnp.where(row_col == col_f, scale, 0.0)
            parts += [(h * 256.0).astype(bf16), h.astype(bf16)]
        return jnp.concatenate(parts, axis=1)

    def arrived(j, spot):
        spots = [spot]
        for n in range(2):
            x_copies[n, j].wait_recv()
            at = 256 * (n + 1)
            hi, lo = halves(xr[n, j, 0:128, :])
            rhs[j, at : at + 128, :] = hi
            rhs[j, at + 128 : at + 256, :] = lo
            got = xr[n, j, 128:136, 0:128].astype(f32)
            spots.append((got[0:1], jnp.exp2(got[1:2])))
        return spots

    def deposit(j, i, spots):
        part = jnp.dot(one_hot(i, spots), rhs[j], preferred_element_type=f32)
        if i < 4:
            at = 128 + i * 256
            if j:
                part = part + sx[at : at + 256, :]
            sx[at : at + 256, :] = part
        else:
            if j:
                part = part + edge[...]
            edge[...] = part

    toward = jnp.where(odd == 0, -1, 1)
    placing(0, ls, 0)
    for i in range(4):
        unpack(0, ls, i)
    relay_copies = []

    def pass_on(i):
        at, size = CHUNKS[i]
        list_copies[i].wait_recv()
        copy = send(
            lr.at[0, pl.ds(at, size)], lr.at[1, pl.ds(at, size)], t_s.at[1, i], t_r.at[1, i], (a, relay)
        )
        copies.append(copy)
        relay_copies.append(copy)

    pass_on(0)
    spot = compact(0, ls)
    placing(1, lr.at[0], toward)
    unpack(1, lr.at[0], 0)
    for i in range(1, 4):
        pass_on(i)
        unpack(1, lr.at[0], i)
    next_spot = compact(1, lr.at[0])
    spots = arrived(0, spot)
    for i in range(5):
        deposit(0, i, spots)
    relay_copies[0].wait_recv()
    placing(2, lr.at[1], -toward)
    unpack(2, lr.at[1], 0)
    for i in range(1, 4):
        relay_copies[i].wait_recv()
        unpack(2, lr.at[1], i)
    last_spot = compact(2, lr.at[1])
    spots = arrived(1, next_spot)
    for i in range(5):
        deposit(1, i, spots)
    spots = arrived(2, last_spot)

    deposit(2, 4, spots)
    z_copies, h_copies, c_copies, o_copies = [], [], [], []
    vc, ec = coded(
        jnp.concatenate(
            [edge[at : at + 16, :] for at in (112, 128 + 112, 0, 128)], axis=0
        )
    )
    info = info_rows(to_row(ec)[0])
    for n in range(2):
        hc[n, 0:32, :] = vc[n * 32 : n * 32 + 32, :]
        hc[n, 32:40, :] = info
        c_copies.append(send(hc.at[n], hcr.at[n], hc_s.at[n], hc_r.at[n], sides_x[n]))

    def banded(shape, out_pos, in_pos):
        apart = in_pos - out_pos
        matrix = jnp.zeros(shape, f32)
        for k in range(2 * REACH + 1):
            matrix = jnp.where(apart == 4 * (k - REACH), TAPS[k], matrix)
        return matrix

    own_x = banded((128, 128), iota((128, 128), 0), iota((128, 128), 1))
    for n, s in ((0, 1), (1, 0)):
        made = jnp.dot(
            own_x, edge[s * 128 : (s + 1) * 128, :], precision=HIGHEST, preferred_element_type=f32
        )
        part_x[s, 0:16, :] = made[0:16, :]
        part_x[s, 16:32, :] = made[112:128, :]
        ve, ee = coded(made[16:112, :])
        hz[n, 0:96, :] = ve
        hz[n, 96:104, :] = info_rows(to_row(ee)[0])
        z_copies.append(send(hz.at[n], hzr.at[n], hz_s.at[n], hz_r.at[n], sides_z[n]))
    for n, i in ((0, 3), (1, 0)):
        deposit(2, i, spots)
        at = COLS if n == 0 else 128
        vx, ex = coded(sx[at : at + 128, :])
        hx[n, 0:128, :] = vx
        hx[n, 128:136, :] = info_rows(to_row(ex)[0])
        h_copies.append(send(hx.at[n], hxr.at[n], hx_s.at[n], hx_r.at[n], sides_x[n]))
    i_out, i_in = iota((32, 32), 0), iota((32, 32), 1)
    far_x = banded(
        (32, 32), jnp.where(i_out < 16, i_out, i_out + 96), jnp.where(i_in < 16, i_in - 16, i_in + 112)
    )
    beyond = []
    for n in range(2):
        c_copies[n].wait_recv()
        scale = jnp.exp2(to_column(hcr[n, 32:33, 0:128].astype(f32)))
        beyond.append(integers(hcr[n, 0:32, :]).astype(f32) * scale[n * 32 : n * 32 + 32])
    outer = []
    for s in range(2):
        rows = jnp.concatenate([v[s * 16 : s * 16 + 16] for v in beyond], axis=0)
        outer.append(
            part_x[s] + jnp.dot(far_x, rows, precision=HIGHEST, preferred_element_type=f32)
        )
    vo, eo = coded(jnp.concatenate(outer, axis=0))
    info = info_rows(to_row(eo)[0])
    for n, s in ((0, 1), (1, 0)):
        ho[n, 0:32, :] = vo[s * 32 : s * 32 + 32, :]
        ho[n, 32:40, :] = info
        o_copies.append(send(ho.at[n], hor.at[n], ho_s.at[n], ho_r.at[n], sides_z[n]))
    copies += z_copies + h_copies + c_copies + o_copies
    deposit(2, 1, spots)
    deposit(2, 2, spots)
    for n in range(2):
        h_copies[n].wait_recv()
    for n in range(2):
        got = hxr[n, 0:128, :]
        scale = jnp.exp2(to_column(hxr[n, 128:129, 0:128].astype(f32)))
        at = 0 if n == 0 else COLS + 128
        sx[at : at + 128, :] = integers(got).astype(f32) * scale

    def taps(term):
        total = term(REACH) * TAPS[REACH]
        for k in range(1, REACH + 1):
            total = total + (term(REACH - k) + term(REACH + k)) * TAPS[REACH + k]
        return total

    EXT = (CZ + 2 * REACH) * CH

    def x_pass(x, _):
        total = taps(lambda k: sx[pl.ds(pl.multiple_of((x + k) * CZ, CZ), CZ), :])
        for c in range(CH):
            ax[pl.ds(x * EXT + 4 * CH + c, CZ, stride=CH), :] = total[:, c * NY : (c + 1) * NY]
        inner = taps(lambda k: ax[pl.ds(x * EXT + 4 * CH + CH * k, (CZ - 8) * CH), :])
        out_ref[x, 4 * CH : (CZ - 4) * CH, :] = inner
        return 0

    lax.fori_loop(0, CX, x_pass, 0)

    def leave(at, size, sem):
        copy = pltpu.make_async_copy(
            out_ref.at[:, pl.ds(at, size)], out_hbm.at[:, pl.ds(at, size)], out_s.at[sem]
        )
        copy.start()
        return copy

    leaving = [leave(4 * CH, (CZ - 8) * CH, 0)]
    for n in range(2):
        z_copies[n].wait_recv()
        scale = jnp.exp2(to_column(hzr[n, 96:97, 0:128].astype(f32)))
        rows = integers(hzr[n, 0:96, :]).astype(f32) * scale[0:96]
        for c in range(CH):
            zx[n, pl.ds(16 * CH + c, 96, stride=CH), :] = rows[:, c * NY : (c + 1) * NY]
    for n in range(2):
        o_copies[n].wait_recv()
        scale = jnp.exp2(to_column(hor[n, 32:33, 0:128].astype(f32)))
        s = 1 - n
        rows = integers(hor[n, 0:32, :]).astype(f32) * scale[s * 32 : s * 32 + 32]
        for half in range(2):
            for c in range(CH):
                zx[n, pl.ds(half * 112 * CH + c, 16, stride=CH), :] = rows[
                    half * 16 : half * 16 + 16, c * NY : (c + 1) * NY
                ]

    W = 4 * CH

    def z_pass(step, _):
        for part in range(4):
            x = step * 4 + part
            for n in range(2):
                at = x * EXT + (0 if n == 0 else (CZ + REACH) * CH)
                ax[pl.ds(pl.multiple_of(at, 8), W), :] = zx[n, pl.ds(pl.multiple_of(x * W, W), W), :]
        for part in range(4):
            x = step * 4 + part
            for z in (0, CZ - REACH):
                total = taps(lambda k: ax[pl.ds(x * EXT + CH * (z + k), W), :])
                out_ref[x, z * CH : z * CH + W, :] = total
        return 0

    lax.fori_loop(0, CX // 4, z_pass, 0)
    leaving += [leave(0, W, 1), leave((CZ - 4) * CH, W, 2)]
    for copy in copies:
        copy.wait_send()
    for copy in leaving:
        copy.wait()


def hand_over(src, dst, held, in_s, out_s):
    part = CX // 8
    came, went = [], []
    for i in range(8):
        rows = pl.ds(i * part, part)
        came.append(pltpu.make_async_copy(src.at[rows], held.at[rows], in_s.at[i]))
        came[i].start()
    for i in range(8):
        rows = pl.ds(i * part, part)
        came[i].wait()
        went.append(pltpu.make_async_copy(held.at[rows], dst.at[rows], out_s.at[i]))
        went[i].start()
    for copy in went:
        copy.wait()


def local(particle_drag, particle_weights, migration_counts, tile_owner, tile_column):
    dma = pltpu.SemaphoreType.DMA
    hbm = pl.BlockSpec(memory_space=pltpu.HBM)
    out = pl.pallas_call(
        kernel,
        out_shape=jax.ShapeDtypeStruct((CX, CZ * CH, NY), f32),
        in_specs=[hbm] * 5,
        out_specs=hbm,
        scratch_shapes=[
            pltpu.SMEM((1, 5), i32),
            pltpu.VMEM((CH, P_SIZE), bf16),
            pltpu.VMEM((P_SIZE, NY), bf16),
            pltpu.VMEM((1, NT), i32),
            pltpu.VMEM((1, NT), i32),
            pltpu.VMEM((512, P_SIZE - MOVED_AT), bf16),
            pltpu.VMEM((CH, P_SIZE), f32),
            pltpu.VMEM((256, F), f32),
            pltpu.VMEM((4, 40, 256), i32),
            pltpu.VMEM((4, 40, 256), i32),
            pltpu.VMEM((LIST, 256), i32),
            pltpu.VMEM((2, LIST, 256), i32),
            pltpu.VMEM((3, NT, NT), bf16),
            pltpu.VMEM((3, NT, 2 * F), bf16),
            pltpu.VMEM((2, 3, 136, 256), i32),
            pltpu.VMEM((2, 3, 136, 256), i32),
            pltpu.VMEM((3, 768, F), bf16),
            pltpu.VMEM((COLS + 256, F), f32),
            pltpu.VMEM((256, F), f32),
            pltpu.VMEM((2, 136, 256), i32),
            pltpu.VMEM((2, 136, 256), i32),
            pltpu.VMEM((2, 104, 256), i32),
            pltpu.VMEM((2, 104, 256), i32),
            pltpu.VMEM((2, 40, 256), i32),
            pltpu.VMEM((2, 40, 256), i32),
            pltpu.VMEM((2, 40, 256), i32),
            pltpu.VMEM((2, 40, 256), i32),
            pltpu.VMEM((2, 32, F), f32),
            pltpu.VMEM((2, 512, NY), f32),
            pltpu.VMEM((CX * (CZ + 2 * REACH) * CH, NY), f32),
            pltpu.VMEM((CX, CZ * CH, NY), f32),
            dma((5,)), dma((3,)),
            dma((4,)), dma((4,)),
            dma((2, 4)), dma((2, 4)),
            dma((2, 3)), dma((2, 3)),
            dma((2,)), dma((2,)),
            dma((2,)), dma((2,)),
            dma((2,)), dma((2,)),
            dma((2,)), dma((2,)),
        ],
        compiler_params=pltpu.CompilerParams(
            collective_id=0, has_side_effects=True, vmem_limit_bytes=56500 * 1024
        ),
        cost_estimate=pl.CostEstimate(
            flops=8_000_000_000, bytes_accessed=3_000_000, transcendentals=0
        ),
        name="deposit_and_filter",
    )(
        migration_counts.reshape(1, 5),
        particle_drag.reshape(CH, P_SIZE),
        particle_weights.reshape(P_SIZE, NY),
        tile_owner.reshape(1, NT),
        tile_column.reshape(1, NT),
    )
    out = pl.pallas_call(
        hand_over,
        out_shape=jax.ShapeDtypeStruct(out.shape, f32),
        in_specs=[hbm],
        out_specs=hbm,
        scratch_shapes=[pltpu.VMEM((CX, CZ * CH, NY), f32), dma((8,)), dma((8,))],
        compiler_params=pltpu.CompilerParams(vmem_limit_bytes=56500 * 1024),
        name="hand_over",
    )(out)
    return out.reshape(CX, CZ, CH, NY)


def solution(mesh):
    in_specs = (
        P("gx", "gz", None, None),
        P("gx", "gz", None, None),
        P("gx", "gz", None),
        P("gx", "gz", None, None),
        P("gx", "gz", None),
    )
    out_specs = P("gx", "gz", None, None)
    return jax.shard_map(local, mesh=mesh, in_specs=in_specs, out_specs=out_specs, check_vma=False)
```
